256 devices in a mesh: shard: 64 (over y, z_lo, x, core), rep: 4 (over z_hi).
Axes of the slice: x: 4, y: 4, z: 8 (z_hi: 4, z_lo: 2; z = z_hi * 2 + z_lo), core: 2. Of those that a mesh axis runs over, the one named last changes fastest.
Arguments:
- pooled_grad: float32 [1024, 4, 64, 256], P('shard', 'rep'), may hold values from -0.8 to 0.8
- bag_lengths: int32 [64, 4, 1024], P('shard', 'rep'), may hold values from 1 to 64, 16384 in all within a row
- row_slots: int32 [64, 4, 16384], P('shard', 'rep'), may hold values from 0 to 511
- id_weights: int32 [64, 4, 16384], P('shard', 'rep'), may hold values from 1 to 32
- touched_rows: float32 [64, 512, 256], P('shard'), may hold values from -6 to 6
- accumulator: float32 [64, 512], P('shard'), may hold values from 0.005 to 0.5
Outputs:
- row_grad: float32 [64, 512, 256], P('shard', 'rep')
- updated_rows: float32 [64, 512, 256], P('shard')
The draws below stay inside these ranges and needn't reach their ends.
Inputs may be any that keep to these rules, and one draw needn't show every extreme that they name: `bag_lengths`: in each table and replica group the bag lengths sum to 16384.
All inputs are finite; a program needn't handle non-finite values.
Results may differ from the reference program's by a relative error of at most 0.0003.
Values sent between devices are 32-bit elements; how exact they have to be, the bound alone decides.
No kernel may reach another device: no remote copies, remote signals or barrier semaphores. Data moves between devices by JAX's collectives and lax.ppermute only.
A program may use at most 64 MiB of HBM per device.

```python
import math
import jax
import jax.numpy as jnp
import numpy as np
from jax import lax

E = 256
MOST = 64
SLOTS = 512
TABLES = 64
REPS = 4
SH_SAMPLES = 1024
ENTRIES = 16384


def with_ends(result, own_key, low, top_value):
    longest = result.shape.index(max(result.shape))
    spots = []
    for shift in (0, 1):
        where = [jax.random.randint(jax.random.fold_in(own_key, axis), (), 0, length) for axis, length in enumerate(result.shape)]
        where[longest] = (where[longest] + shift) % result.shape[longest]
        spots.append(tuple(where))
    return result.at[spots[0]].set(low).at[spots[1]].set(top_value)


def level_of(rng, extent, cuts, smallest, top_value):
    factor_of, own = 1.0, jax.random.fold_in(rng, 6)
    for dim, parts in cuts:
        heights = jnp.exp(jax.random.uniform(jax.random.fold_in(own, dim), (parts,), jnp.float32, smallest / len(cuts), top_value / len(cuts)))
        factor_of = factor_of * jnp.repeat(heights, extent[dim] // parts).reshape([-1 if axis == dim else 1 for axis in range(len(extent))])
    return factor_of


def rank_table(count, slope):
    portions = [(1 << 20) // math.isqrt(rank ** slope) + 1 for rank in range(1, count + 1)]
    scale = 1 + sum(portions) // (1 << 30)
    return np.cumsum(np.array([max(1, weight // scale) for weight in portions]))


def ranked(stream_key, dims, amount, lean):
    table = rank_table(amount, lean)
    pick = jax.random.randint(jax.random.fold_in(stream_key, 1), dims, 0, int(table[amount - 1]))
    grade = jnp.searchsorted(jnp.asarray(table, jnp.int32), pick, side="right")
    return jax.random.permutation(jax.random.fold_in(stream_key, 2), amount)[grade].astype(jnp.int32)


def length_profile(count, total, reach, skew):
    loads = [(1 << 20) // math.isqrt(standing ** skew) + 1 for standing in range(2, count + 1)]
    surplus, holding = total - reach - (count - 1), [1] * (count - 1)
    while surplus > 0:
        movable = [i for i in range(count - 1) if holding[i] < reach]
        mass, remaining = sum([loads[i] for i in movable]), surplus
        for i in movable:
            more = min(reach - holding[i], max(1, remaining * loads[i] // mass), surplus)
            holding[i] = holding[i] + more
            surplus = surplus - more
    return np.array([reach] + holding)


def uneven_parts(rng, number_of, total, bound, slope):
    if number_of == 2:
        one = jax.random.randint(rng, (), max(1, total - bound), min(bound, total - 1) + 1)
        return jnp.stack([one, total - one])
    sizes = jnp.asarray(length_profile(number_of, total, bound, slope), jnp.int32)
    pairs = (number_of - 1) // 2
    giver, sink = sizes[1:1 + 2 * pairs:2], sizes[2:2 + 2 * pairs:2]
    slack = jnp.minimum(giver - 1, bound - sink)
    moved = jax.random.randint(jax.random.fold_in(rng, 1), (pairs,), 0, 1 << 20) % (slack + 1)
    sizes = sizes.at[1:1 + 2 * pairs:2].set(giver - moved).at[2:2 + 2 * pairs:2].set(sink + moved)
    return sizes[jax.random.permutation(jax.random.fold_in(rng, 2), number_of)]


def scatter_about(key, extent, spread, limit, cuts=(), kind=jnp.bfloat16):
    result = spread * jax.random.normal(key, extent, jnp.float32)
    if cuts:
        result = result * level_of(key, extent, cuts, -0.22, 0.18)
    return jnp.clip(result, -limit, limit).astype(kind)


def setup_inputs(seed: int = 0) -> dict:
    key_of = jax.random.split(jax.random.key(seed), 7)
    pooled_grad = scatter_about(key_of[0], (SH_SAMPLES, REPS, TABLES, E), 0.1, 0.8, ((0, 64), (1, 4)), jnp.float32)
    bag_lengths = jax.vmap(lambda own: uneven_parts(own, SH_SAMPLES, ENTRIES, MOST, 2))(jax.random.split(key_of[1], TABLES * REPS)).reshape((TABLES, REPS, SH_SAMPLES)).astype(jnp.int32)
    row_slots = with_ends(ranked(key_of[2], (TABLES, REPS, ENTRIES), SLOTS, 2), jax.random.fold_in(key_of[2], 3), 0, SLOTS - 1).astype(jnp.int32)
    id_weights = with_ends(jax.random.randint(key_of[3], (TABLES, REPS, ENTRIES), 1, 33), jax.random.fold_in(key_of[3], 1), 1, 32).astype(jnp.int32)
    touched_rows = scatter_about(key_of[4], (TABLES, SLOTS, E), 1.0, 6.0, ((0, 64),), jnp.float32)
    accumulator = jnp.clip(jnp.exp(math.log(0.5) - 4.6051702 * jax.random.uniform(key_of[5], (TABLES, SLOTS), jnp.float32) ** level_of(key_of[5], (TABLES, SLOTS), ((0, 64),), -0.2, 0.2)), 0.005, 0.5)
    return {"pooled_grad": pooled_grad, "bag_lengths": bag_lengths, "row_slots": row_slots, "id_weights": id_weights, "touched_rows": touched_rows, "accumulator": accumulator}


learn_rate = 0.5

def one_table(index, pooled_grad, bag_lengths, row_slots, id_weights):
    total = jnp.zeros((SLOTS, E), jnp.float32)
    positions = jnp.arange(ENTRIES, dtype=jnp.int32)
    for group in range(REPS):
        ends = jnp.cumsum(bag_lengths[index, group]).astype(jnp.int32)
        bags = jnp.searchsorted(ends, positions, side='right').astype(jnp.int32)
        column = pooled_grad[:, group, index]
        scaled = id_weights[index, group].astype(jnp.float32) * 0.0625
        picked = jnp.take(column, bags, axis=0) * scaled[:, None]
        total = total + jax.ops.segment_sum(picked, row_slots[index, group], num_segments=SLOTS)
    return total

def reference(pooled_grad, bag_lengths, row_slots, id_weights, touched_rows, accumulator):
    grads = lax.map(lambda index: one_table(index, pooled_grad, bag_lengths, row_slots, id_weights), jnp.arange(TABLES, dtype=jnp.int32))
    new_state = accumulator + lax.optimization_barrier(jnp.mean(grads * grads, axis=-1))
    updated = touched_rows - learn_rate * grads / (jnp.sqrt(new_state)[..., None] + 1e-08)
    return (grads, updated)
```

```python
import jax
import jax.numpy as jnp
from jax import lax
from jax.experimental import pallas as pl
from jax.experimental.pallas import tpu as pltpu
from jax.sharding import PartitionSpec as P

learn_rate = 0.5
span = 512
window = 256
VMEM = pltpu.VMEM
SMEM = pltpu.SMEM


def tally_kernel(edges, starts_ref, ends_ref, slots_ref, weights_ref, high_ref, low_ref, total):
    height = total.shape[0]
    slot_ids = lax.broadcasted_iota(jnp.int32, (height, span), 0)
    offsets = lax.broadcasted_iota(jnp.int32, (span, window), 0)
    for part in range(high_ref.shape[1] // window):
        columns = pl.ds(part * window, window)
        starts = starts_ref[:, columns]
        ends = ends_ref[:, columns]
        total[...] = jnp.zeros_like(total)

        def add_block(block, carry):
            base = pl.multiple_of(block * span, span)
            slots = slots_ref[:, pl.ds(base, span)]
            weights = weights_ref[:, pl.ds(base, span)]
            chosen = jnp.where(slot_ids == slots, weights.astype(jnp.float32), 0.0)
            member = (offsets >= starts - base) & (offsets < ends - base)
            total[...] += jnp.dot(
                chosen.astype(jnp.bfloat16),
                jnp.where(member, 1.0, 0.0).astype(jnp.bfloat16),
                preferred_element_type=jnp.float32,
            )
            return carry

        first = edges[part] // span
        last = (edges[part + 1] + span - 1) // span
        lax.fori_loop(first, last, add_block, 0)
        high = total[...].astype(jnp.bfloat16)
        high_ref[:, columns] = high
        low_ref[:, columns] = (total[...] - high.astype(jnp.float32)).astype(jnp.bfloat16)


def tallies(lengths, slots, weights, height):
    bags = lengths.shape[1]
    ends = jnp.cumsum(lengths, axis=1)
    starts = ends - lengths
    edges = jnp.concatenate([starts[0, ::window], ends[0, -1:]])
    shape = jax.ShapeDtypeStruct((height, bags), jnp.bfloat16)
    return pl.pallas_call(
        tally_kernel,
        out_shape=(shape, shape),
        in_specs=[pl.BlockSpec(memory_space=SMEM)] + [pl.BlockSpec(memory_space=VMEM)] * 4,
        out_specs=(pl.BlockSpec(memory_space=VMEM),) * 2,
        scratch_shapes=[pltpu.VMEM((height, window), jnp.float32)],
        compiler_params=pltpu.CompilerParams(vmem_limit_bytes=24 << 20),
        cost_estimate=pl.CostEstimate(
            flops=2 * 35 * height * span * window, bytes_accessed=2 << 20, transcendentals=0
        ),
    )(edges, starts, ends, slots, weights)


def rows_kernel(picks, high_ref, low_ref, arrived_ref, out_ref):
    wide = arrived_ref[...]
    upper = wide.astype(jnp.bfloat16)
    lower = (wide - upper.astype(jnp.float32)).astype(jnp.bfloat16)
    count = out_ref.shape[1]
    for place in range(out_ref.shape[0]):
        rows = pl.ds(pl.multiple_of(picks[place] * count, count), count)
        high = high_ref[rows, :]
        low = low_ref[rows, :]
        dot = lambda a, b: jnp.dot(a, b, preferred_element_type=jnp.float32)
        out_ref[place] = (dot(high, lower) + dot(low, upper) + dot(high, upper)) * 0.0625


def grad_rows(picks, high, low, arrived, count):
    width = arrived.shape[1]
    return pl.pallas_call(
        rows_kernel,
        out_shape=jax.ShapeDtypeStruct((picks.shape[0], count, width), jnp.float32),
        in_specs=[pl.BlockSpec(memory_space=SMEM)] + [pl.BlockSpec(memory_space=VMEM)] * 3,
        out_specs=pl.BlockSpec(memory_space=VMEM),
        compiler_params=pltpu.CompilerParams(vmem_limit_bytes=24 << 20),
        cost_estimate=pl.CostEstimate(
            flops=6 * picks.shape[0] * count * width * high.shape[1],
            bytes_accessed=4 << 20,
            transcendentals=0,
        ),
    )(picks, high, low, arrived)


def adagrad_kernel(picks, mine_ref, other_ref, rows_ref, state_ref, grad_ref, fresh_ref):
    count = mine_ref.shape[1]
    for place in range(2):
        rows = pl.ds(pl.multiple_of(picks[place] * count, count), count)
        grads = mine_ref[place] + other_ref[1 - place]
        if place == 0:
            grad_ref[...] = grads
        state = state_ref[rows, :] + jnp.mean(grads * grads, axis=-1, keepdims=True)
        fresh_ref[place] = rows_ref[rows, :] - learn_rate * grads / (jnp.sqrt(state) + 1e-08)


def adagrad(picks, mine, other, rows, state):
    _, count, width = mine.shape
    return pl.pallas_call(
        adagrad_kernel,
        out_shape=(
            jax.ShapeDtypeStruct((count, width), jnp.float32),
            jax.ShapeDtypeStruct((2, count, width), jnp.float32),
        ),
        in_specs=[pl.BlockSpec(memory_space=SMEM)] + [pl.BlockSpec(memory_space=VMEM)] * 4,
        out_specs=(pl.BlockSpec(memory_space=VMEM),) * 2,
        compiler_params=pltpu.CompilerParams(vmem_limit_bytes=16 << 20),
    )(picks, mine, other, rows, state)


def per_device(pooled_grad, bag_lengths, row_slots, id_weights, touched_rows, accumulator):
    reps = lax.axis_size("rep")
    shards = lax.axis_size("shard")
    height = touched_rows.shape[1]
    count = height // reps
    rep = lax.axis_index("rep")
    core = lax.axis_index("shard") % 2
    near = jnp.where(core == 0, 1, 3)
    keep = jnp.stack([rep, rep ^ (near ^ 2)])
    give = jnp.stack([rep ^ near, rep ^ 2])

    def swap(array, step):
        pairs = []
        for shard in range(shards):
            turn = 1 if (shard + step) % 2 == 0 else 3
            pairs += [(shard * reps + r, shard * reps + (r ^ turn)) for r in range(reps)]
        return lax.ppermute(array, ("shard", "rep"), pairs)

    arrived = lax.all_to_all(pooled_grad, "shard", split_axis=2, concat_axis=0, tiled=True)
    arrived = arrived[:, 0, 0]
    high, low = tallies(bag_lengths[0], row_slots[0], id_weights[0], height)
    sent = swap(grad_rows(give, high, low, arrived, count), 0)
    mine = grad_rows(keep, high, low, arrived, count) + sent
    other = swap(mine, 1)
    grad, fresh = adagrad(keep, mine, other, touched_rows[0], accumulator.reshape(height, 1))
    far = swap(fresh, 0)
    updated = jnp.zeros((reps, count, touched_rows.shape[2]), jnp.float32)
    for place in range(2):
        updated = lax.dynamic_update_index_in_dim(updated, fresh[place], keep[place], 0)
    for place in range(2):
        updated = lax.dynamic_update_index_in_dim(updated, far[place], give[place], 0)
    return grad[None], updated.reshape(touched_rows.shape)


def solution(mesh):
    placed = (
        P("shard", "rep", None, None),
        P("shard", "rep", None),
        P("shard", "rep", None),
        P("shard", "rep", None),
        P("shard", None, None),
        P("shard", None),
    )
    return jax.shard_map(
        per_device,
        mesh=mesh,
        in_specs=placed,
        out_specs=(P("shard", "rep", None), P("shard", None, None)),
        check_vma=False,
    )
```

```python
import jax
import jax.numpy as jnp
from jax import lax
from jax.experimental import pallas as pl
from jax.experimental.pallas import tpu as pltpu
from jax.sharding import PartitionSpec as P

learn_rate = 0.5
span = 1024
block = 256
window = 256
VMEM = pltpu.VMEM
SMEM = pltpu.SMEM


def tally_kernel(edges, starts_ref, ends_ref, slots_ref, weights_ref, high_ref, low_ref, total):
    height = total.shape[0]
    narrow = jnp.bfloat16
    half = height // 2

    def coded(slots):
        return jnp.where(slots < half, slots, half - 1 - slots).astype(jnp.float32).astype(narrow)

    slot_ids = coded(lax.broadcasted_iota(jnp.int32, (height, block), 0))
    offsets = lax.broadcasted_iota(jnp.int32, (block, window), 0).astype(jnp.float32).astype(narrow)
    zero = jnp.zeros((), narrow)
    one = jnp.ones((), narrow)
    for part in range(high_ref.shape[1] // window):
        columns = pl.ds(part * window, window)
        starts = starts_ref[:, columns]
        ends = ends_ref[:, columns]
        total[...] = jnp.zeros_like(total)

        def add_span(step, carry):
            added = jnp.zeros_like(total)
            for piece in range(span // block):
                base = pl.multiple_of(step * span + piece * block, block)

                def local(bounds):
                    return jnp.clip(bounds - base, 0, block).astype(jnp.float32).astype(narrow)

                codes = coded(slots_ref[:, pl.ds(base, block)])
                weights = weights_ref[:, pl.ds(base, block)].astype(jnp.float32).astype(narrow)
                chosen = jnp.where(slot_ids == codes, weights, zero)
                member = (offsets >= local(starts)) & (offsets < local(ends))
                added += jnp.dot(
                    chosen, jnp.where(member, one, zero), preferred_element_type=jnp.float32
                )
            total[...] += added
            return carry

        first = edges[part] // span
        last = (edges[part + 1] + span - 1) // span
        lax.fori_loop(first, last, add_span, 0)
        high = total[...].astype(narrow)
        high_ref[:, columns] = high
        low_ref[:, columns] = (total[...] - high.astype(jnp.float32)).astype(narrow)


def spec(space):
    return pl.BlockSpec(memory_space=space)


def limit(mebibytes):
    return pltpu.CompilerParams(vmem_limit_bytes=mebibytes << 20)


def tallies(lengths, slots, weights, height):
    bags = lengths.shape[1]
    ends = jnp.cumsum(lengths, axis=1)
    starts = ends - lengths
    edges = jnp.concatenate([starts[0, ::window], ends[0, -1:]])
    shape = jax.ShapeDtypeStruct((height, bags), jnp.bfloat16)
    return pl.pallas_call(
        tally_kernel,
        out_shape=(shape, shape),
        in_specs=[spec(SMEM)] + [spec(VMEM)] * 4,
        out_specs=(spec(VMEM),) * 2,
        scratch_shapes=[pltpu.VMEM((height, window), jnp.float32)],
        compiler_params=limit(10),
        cost_estimate=pl.CostEstimate(
            flops=2 * 35 * height * 512 * window, bytes_accessed=2 << 20, transcendentals=0
        ),
    )(edges, starts, ends, slots, weights)


def rows_kernel(picks, high_ref, low_ref, arrived_ref, *out_refs):
    wide = arrived_ref[...]
    upper = wide.astype(jnp.bfloat16)
    lower = (wide - upper.astype(jnp.float32)).astype(jnp.bfloat16)
    dot = lambda a, b: jnp.dot(a, b, preferred_element_type=jnp.float32)
    for place, out_ref in enumerate(out_refs):
        count = out_ref.shape[0]
        rows = pl.ds(pl.multiple_of(picks[place] * count, count), count)
        high = high_ref[rows, :]
        low = low_ref[rows, :]
        out_ref[...] = (dot(high, lower) + dot(low, upper) + dot(high, upper)) * 0.0625


def grad_rows(picks, high, low, arrived, count):
    width = arrived.shape[1]
    shape = jax.ShapeDtypeStruct((count, width), jnp.float32)
    return pl.pallas_call(
        rows_kernel,
        out_shape=(shape, shape),
        in_specs=[spec(SMEM)] + [spec(VMEM)] * 3,
        out_specs=(spec(VMEM),) * 2,
        compiler_params=limit(10),
        cost_estimate=pl.CostEstimate(
            flops=12 * count * width * high.shape[1], bytes_accessed=3 << 20, transcendentals=0
        ),
    )(picks, high, low, arrived)


def add_kernel(one_ref, two_ref, out_ref):
    out_ref[...] = one_ref[...] + two_ref[...]


def added(one, two):
    return pl.pallas_call(
        add_kernel,
        out_shape=jax.ShapeDtypeStruct(one.shape, one.dtype),
        in_specs=[spec(VMEM)] * 2,
        out_specs=spec(VMEM),
        compiler_params=limit(2),
    )(one, two)


def adagrad_kernel(pick, mine_ref, other_ref, rows_ref, state_ref, grad_ref, fresh_ref):
    count = mine_ref.shape[0]
    rows = pl.ds(pl.multiple_of(pick[0] * count, count), count)
    grads = mine_ref[...] + other_ref[...]
    grad_ref[...] = grads
    state = state_ref[rows, :] + jnp.mean(grads * grads, axis=-1, keepdims=True)
    fresh_ref[...] = rows_ref[rows, :] - learn_rate * grads / (jnp.sqrt(state) + 1e-08)


def adagrad(pick, mine, other, rows, state):
    shape = jax.ShapeDtypeStruct(mine.shape, jnp.float32)
    return pl.pallas_call(
        adagrad_kernel,
        out_shape=(shape, shape),
        in_specs=[spec(SMEM)] + [spec(VMEM)] * 4,
        out_specs=(spec(VMEM),) * 2,
        compiler_params=limit(4),
    )(pick, mine, other, rows, state)


def per_device(pooled_grad, bag_lengths, row_slots, id_weights, touched_rows, accumulator):
    reps = lax.axis_size("rep")
    shards = lax.axis_size("shard")
    height = touched_rows.shape[1]
    count = height // reps
    rep = lax.axis_index("rep")
    core = lax.axis_index("shard") % 2
    near = jnp.where(core == 0, 1, 3)

    def ordered(one, two):
        return jnp.stack([jnp.minimum(one, two), jnp.maximum(one, two)])

    keep = ordered(rep, rep ^ (near ^ 2))
    give = ordered(rep ^ near, rep ^ 2)

    def swap(array, step):
        pairs = []
        for shard in range(shards):
            turn = 1 if (shard + step) % 2 == 0 else 3
            pairs += [(shard * reps + r, shard * reps + (r ^ turn)) for r in range(reps)]
        return lax.ppermute(array, ("shard", "rep"), pairs)

    by_table = jnp.transpose(pooled_grad[:, 0], (1, 0, 2))
    arrived = lax.all_to_all(by_table, "shard", 0, 0, tiled=True)
    arrived = arrived.reshape(-1, arrived.shape[2])
    high, low = tallies(bag_lengths[0], row_slots[0], id_weights[0], height)
    state = accumulator.reshape(height, 1)
    given = grad_rows(give, high, low, arrived, count)
    sent = [swap(piece, 0) for piece in given]
    kept = grad_rows(keep, high, low, arrived, count)
    mine = [added(kept[k], sent[k]) for k in range(2)]
    other = [swap(piece, 1) for piece in mine]
    grads, fresh = zip(
        *[adagrad(keep[k : k + 1], mine[k], other[k], touched_rows[0], state) for k in range(2)]
    )
    far = [swap(piece, 0) for piece in fresh]
    grad = jnp.where(rep == keep[0], grads[0], grads[1])
    updated = jnp.zeros((reps, count, touched_rows.shape[2]), jnp.float32)
    for k in range(2):
        updated = lax.dynamic_update_index_in_dim(updated, fresh[k], keep[k], 0)
    for k in range(2):
        updated = lax.dynamic_update_index_in_dim(updated, far[k], give[k], 0)
    return grad[None], updated.reshape(touched_rows.shape)


def solution(mesh):
    placed = (
        P("shard", "rep", None, None),
        P("shard", "rep", None),
        P("shard", "rep", None),
        P("shard", "rep", None),
        P("shard", None, None),
        P("shard", None),
    )
    return jax.shard_map(
        per_device,
        mesh=mesh,
        in_specs=placed,
        out_specs=(P("shard", "rep", None), P("shard", None, None)),
        check_vma=False,
    )
```

```python
import jax
import jax.numpy as jnp
from jax import lax
from jax.experimental import pallas as pl
from jax.experimental.pallas import tpu as pltpu
from jax.sharding import PartitionSpec as P

learn_rate = 0.5
span = 1024
block = 256
window = 256
VMEM = pltpu.VMEM
SMEM = pltpu.SMEM


def tally_kernel(edges, starts_ref, ends_ref, slots_ref, weights_ref, high_ref, low_ref, total):
    height = total.shape[0]
    narrow = jnp.bfloat16
    half = height // 2

    def coded(slots):
        return jnp.where(slots < half, slots, half - 1 - slots).astype(jnp.float32).astype(narrow)

    slot_ids = coded(lax.broadcasted_iota(jnp.int32, (height, block), 0))
    offsets = lax.broadcasted_iota(jnp.int32, (block, window), 0).astype(jnp.float32).astype(narrow)
    zero = jnp.zeros((), narrow)
    one = jnp.ones((), narrow)
    for part in range(high_ref.shape[1] // window):
        columns = pl.ds(part * window, window)
        starts = starts_ref[:, columns]
        ends = ends_ref[:, columns]
        total[...] = jnp.zeros_like(total)

        def add_span(step, carry):
            added = jnp.zeros_like(total)
            for piece in range(span // block):
                base = pl.multiple_of(step * span + piece * block, block)

                def local(bounds):
                    return jnp.clip(bounds - base, 0, block).astype(jnp.float32).astype(narrow)

                codes = coded(slots_ref[:, pl.ds(base, block)])
                weights = weights_ref[:, pl.ds(base, block)].astype(jnp.float32).astype(narrow)
                chosen = jnp.where(slot_ids == codes, weights, zero)
                member = (offsets >= local(starts)) & (offsets < local(ends))
                added += jnp.dot(
                    chosen, jnp.where(member, one, zero), preferred_element_type=jnp.float32
                )
            total[...] += added
            return carry

        first = edges[part] // span
        last = (edges[part + 1] + span - 1) // span
        lax.fori_loop(first, last, add_span, 0)
        high = total[...].astype(narrow)
        high_ref[:, columns] = high
        low_ref[:, columns] = (total[...] - high.astype(jnp.float32)).astype(narrow)


def spec(space):
    return pl.BlockSpec(memory_space=space)


def limit(mebibytes):
    return pltpu.CompilerParams(vmem_limit_bytes=mebibytes << 20)


def tallies(lengths, slots, weights, height):
    bags = lengths.shape[1]
    ends = jnp.cumsum(lengths, axis=1)
    starts = ends - lengths
    edges = jnp.concatenate([starts[0, ::window], ends[0, -1:]])
    shape = jax.ShapeDtypeStruct((height, bags), jnp.bfloat16)
    return pl.pallas_call(
        tally_kernel,
        out_shape=(shape, shape),
        in_specs=[spec(SMEM)] + [spec(VMEM)] * 4,
        out_specs=(spec(VMEM),) * 2,
        scratch_shapes=[pltpu.VMEM((height, window), jnp.float32)],
        compiler_params=limit(10),
        cost_estimate=pl.CostEstimate(
            flops=2 * 35 * height * 512 * window, bytes_accessed=2 << 20, transcendentals=0
        ),
    )(edges, starts, ends, slots, weights)


def by_table_kernel(samples_ref, tables_ref, taken, placed, in_sems, out_sems):
    steps, _, each, lanes = taken.shape
    halves = 2
    groups = steps // halves
    count = placed.shape[1]

    def fetch(step):
        group, half = step // halves, step % halves
        rows = samples_ref.at[:, 0, pl.ds(each * group, each), pl.ds(lanes * half, lanes)]
        return pltpu.make_async_copy(rows, taken.at[step], in_sems.at[step])

    def put(group):
        tables = pl.ds(each * group, each)
        return pltpu.make_async_copy(placed.at[tables], tables_ref.at[tables], out_sems.at[group])

    for step in range(steps):
        fetch(step).start()
    for step in range(steps):
        group, half = step // halves, step % halves
        fetch(step).wait()
        rows = taken.at[step].reshape(count * each, lanes)
        for table in range(each):
            picked = rows[pl.ds(table, count, stride=each), :]
            placed[each * group + table, :, lanes * half : lanes * (half + 1)] = picked
        if half == halves - 1:
            put(group).start()
    for group in range(groups):
        put(group).wait()


def by_table(samples):
    count, _, tables, width = samples.shape
    groups, lanes = tables // 8, width // 2
    return pl.pallas_call(
        by_table_kernel,
        out_shape=jax.ShapeDtypeStruct((tables, count, width), jnp.float32),
        in_specs=[spec(pltpu.HBM)],
        out_specs=spec(pltpu.HBM),
        scratch_shapes=[
            pltpu.VMEM((2 * groups, count, 8, lanes), jnp.float32),
            pltpu.VMEM((tables, count, width), jnp.float32),
            pltpu.SemaphoreType.DMA((2 * groups,)),
            pltpu.SemaphoreType.DMA((groups,)),
        ],
        compiler_params=limit(63),
    )(samples)


def chunk_rows(place, high_ref, low_ref, upper, lower, count):
    rows = pl.ds(pl.multiple_of(place * count, count), count)
    high = high_ref[rows, :]
    low = low_ref[rows, :]
    dot = lambda a, b: jnp.dot(a, b, preferred_element_type=jnp.float32)
    both = dot(jnp.concatenate([high, low]), upper)
    return (dot(high, lower) + both[count:] + both[:count]) * 0.0625


def first_kernel(picks, high_ref, low_ref, arrived_ref, upper_ref, lower_ref, *out_refs):
    wide = arrived_ref[...]
    upper = wide.astype(jnp.bfloat16)
    lower = (wide - upper.astype(jnp.float32)).astype(jnp.bfloat16)
    upper_ref[...] = upper
    lower_ref[...] = lower
    for place, out_ref in enumerate(out_refs):
        out_ref[...] = chunk_rows(picks[place], high_ref, low_ref, upper, lower, out_ref.shape[0])


def rows_kernel(picks, high_ref, low_ref, upper_ref, lower_ref, *out_refs):
    upper = upper_ref[...]
    lower = lower_ref[...]
    for place, out_ref in enumerate(out_refs):
        out_ref[...] = chunk_rows(picks[place], high_ref, low_ref, upper, lower, out_ref.shape[0])


def first_rows(picks, high, low, arrived, count):
    bags, width = arrived.shape
    chunks = picks.shape[0]
    part = jax.ShapeDtypeStruct((bags, width), jnp.bfloat16)
    shape = jax.ShapeDtypeStruct((count, width), jnp.float32)
    return pl.pallas_call(
        first_kernel,
        out_shape=(part, part) + (shape,) * chunks,
        in_specs=[spec(SMEM)] + [spec(VMEM)] * 3,
        out_specs=(spec(VMEM),) * (2 + chunks),
        compiler_params=limit(10),
        cost_estimate=pl.CostEstimate(
            flops=6 * chunks * count * width * bags, bytes_accessed=3 << 20, transcendentals=0
        ),
    )(picks, high, low, arrived)


def grad_rows(picks, high, low, upper, lower, count):
    bags, width = upper.shape
    chunks = picks.shape[0]
    shape = jax.ShapeDtypeStruct((count, width), jnp.float32)
    return pl.pallas_call(
        rows_kernel,
        out_shape=(shape,) * chunks,
        in_specs=[spec(SMEM)] + [spec(VMEM)] * 4,
        out_specs=(spec(VMEM),) * chunks,
        compiler_params=limit(10),
        cost_estimate=pl.CostEstimate(
            flops=6 * chunks * count * width * bags, bytes_accessed=3 << 20, transcendentals=0
        ),
    )(picks, high, low, upper, lower)


def add_kernel(one_ref, two_ref, out_ref):
    out_ref[...] = one_ref[...] + two_ref[...]


def added(one, two):
    return pl.pallas_call(
        add_kernel,
        out_shape=jax.ShapeDtypeStruct(one.shape, one.dtype),
        in_specs=[spec(VMEM)] * 2,
        out_specs=spec(VMEM),
        compiler_params=limit(2),
    )(one, two)


def adagrad_kernel(pick, mine_ref, other_ref, rows_ref, state_ref, grad_ref, fresh_ref):
    count = mine_ref.shape[0]
    rows = pl.ds(pl.multiple_of(pick[0] * count, count), count)
    grads = mine_ref[...] + other_ref[...]
    grad_ref[...] = grads
    state = state_ref[rows, :] + jnp.mean(grads * grads, axis=-1, keepdims=True)
    fresh_ref[...] = rows_ref[rows, :] - learn_rate * grads / (jnp.sqrt(state) + 1e-08)


def adagrad(pick, mine, other, rows, state):
    shape = jax.ShapeDtypeStruct(mine.shape, jnp.float32)
    return pl.pallas_call(
        adagrad_kernel,
        out_shape=(shape, shape),
        in_specs=[spec(SMEM)] + [spec(VMEM)] * 4,
        out_specs=(spec(VMEM),) * 2,
        compiler_params=limit(4),
    )(pick, mine, other, rows, state)


def per_device(pooled_grad, bag_lengths, row_slots, id_weights, touched_rows, accumulator):
    reps = lax.axis_size("rep")
    shards = lax.axis_size("shard")
    height = touched_rows.shape[1]
    count = height // reps
    rep = lax.axis_index("rep")
    core = lax.axis_index("shard") % 2
    near = jnp.where(core == 0, 1, 3)

    def ordered(one, two):
        return jnp.stack([jnp.minimum(one, two), jnp.maximum(one, two)])

    keep = ordered(rep, rep ^ (near ^ 2))
    give = ordered(rep ^ near, rep ^ 2)

    def swap(array, step):
        pairs = []
        for shard in range(shards):
            turn = 1 if (shard + step) % 2 == 0 else 3
            pairs += [(shard * reps + r, shard * reps + (r ^ turn)) for r in range(reps)]
        return lax.ppermute(array, ("shard", "rep"), pairs)

    arrived = lax.all_to_all(by_table(pooled_grad), "shard", 0, 0, tiled=True)
    arrived = arrived.reshape(-1, arrived.shape[2])
    high, low = tallies(bag_lengths[0], row_slots[0], id_weights[0], height)
    state = accumulator.reshape(height, 1)
    upper, lower, two = first_rows(give[1:], high, low, arrived, count)
    (one,) = grad_rows(give[:1], high, low, upper, lower, count)
    sent = [swap(one, 0), swap(two, 0)]
    kept = grad_rows(keep, high, low, upper, lower, count)
    mine = [added(kept[k], sent[k]) for k in range(2)]
    other = [swap(piece, 1) for piece in mine]
    grads, fresh = zip(
        *[adagrad(keep[k : k + 1], mine[k], other[k], touched_rows[0], state) for k in range(2)]
    )
    far = [swap(piece, 0) for piece in fresh]
    grad = jnp.where(rep == keep[0], grads[0], grads[1])
    updated = jnp.zeros((reps, count, touched_rows.shape[2]), jnp.float32)
    for k in range(2):
        updated = lax.dynamic_update_index_in_dim(updated, fresh[k], keep[k], 0)
    for k in range(2):
        updated = lax.dynamic_update_index_in_dim(updated, far[k], give[k], 0)
    return grad[None], updated.reshape(touched_rows.shape)


def solution(mesh):
    placed = (
        P("shard", "rep", None, None),
        P("shard", "rep", None),
        P("shard", "rep", None),
        P("shard", "rep", None),
        P("shard", None, None),
        P("shard", None),
    )
    return jax.shard_map(
        per_device,
        mesh=mesh,
        in_specs=placed,
        out_specs=(P("shard", "rep", None), P("shard", None, None)),
        check_vma=False,
    )
```

```python
import jax
import jax.numpy as jnp
from jax import lax
from jax.experimental import pallas as pl
from jax.experimental.pallas import tpu as pltpu
from jax.sharding import PartitionSpec as P

learn_rate = 0.5
span = 1024
block = 256
window = 256
VMEM = pltpu.VMEM
SMEM = pltpu.SMEM


def tally_kernel(edges, starts_ref, ends_ref, slots_ref, weights_ref, high_ref, low_ref, total):
    height = total.shape[0]
    narrow = jnp.bfloat16
    half = height // 2

    def coded(slots):
        return jnp.where(slots < half, slots, half - 1 - slots).astype(jnp.float32).astype(narrow)

    slot_ids = coded(lax.broadcasted_iota(jnp.int32, (height, block), 0))
    offsets = lax.broadcasted_iota(jnp.int32, (block, window), 0).astype(jnp.float32).astype(narrow)
    zero = jnp.zeros((), narrow)
    one = jnp.ones((), narrow)
    for part in range(high_ref.shape[1] // window):
        columns = pl.ds(part * window, window)
        starts = starts_ref[:, columns]
        ends = ends_ref[:, columns]
        total[...] = jnp.zeros_like(total)

        def add_span(step, carry):
            added = jnp.zeros_like(total)
            for piece in range(span // block):
                base = pl.multiple_of(step * span + piece * block, block)

                def local(bounds):
                    return jnp.clip(bounds - base, 0, block).astype(jnp.float32).astype(narrow)

                codes = coded(slots_ref[:, pl.ds(base, block)])
                weights = weights_ref[:, pl.ds(base, block)].astype(jnp.float32).astype(narrow)
                chosen = jnp.where(slot_ids == codes, weights, zero)
                member = (offsets >= local(starts)) & (offsets < local(ends))
                added += jnp.dot(
                    chosen, jnp.where(member, one, zero), preferred_element_type=jnp.float32
                )
            total[...] += added
            return carry

        first = edges[part] // span
        last = (edges[part + 1] + span - 1) // span
        lax.fori_loop(first, last, add_span, 0)
        high = total[...].astype(narrow)
        high_ref[:, columns] = high
        low_ref[:, columns] = (total[...] - high.astype(jnp.float32)).astype(narrow)


def spec(space):
    return pl.BlockSpec(memory_space=space)


def limit(mebibytes):
    return pltpu.CompilerParams(vmem_limit_bytes=mebibytes << 20)


def tallies(lengths, slots, weights, height):
    bags = lengths.shape[1]
    ends = jnp.cumsum(lengths, axis=1)
    starts = ends - lengths
    edges = jnp.concatenate([starts[0, ::window], ends[0, -1:]])
    shape = jax.ShapeDtypeStruct((height, bags), jnp.bfloat16)
    return pl.pallas_call(
        tally_kernel,
        out_shape=(shape, shape),
        in_specs=[spec(SMEM)] + [spec(VMEM)] * 4,
        out_specs=(spec(VMEM),) * 2,
        scratch_shapes=[pltpu.VMEM((height, window), jnp.float32)],
        compiler_params=limit(10),
        cost_estimate=pl.CostEstimate(
            flops=2 * 35 * height * 512 * window, bytes_accessed=2 << 20, transcendentals=0
        ),
    )(edges, starts, ends, slots, weights)


def by_table_kernel(samples_ref, tables_ref, taken, placed, in_sems, out_sems):
    steps, _, each, lanes = taken.shape
    halves = 2
    groups = steps // halves
    count = placed.shape[1]

    def fetch(step):
        group, half = step // halves, step % halves
        rows = samples_ref.at[:, 0, pl.ds(each * group, each), pl.ds(lanes * half, lanes)]
        return pltpu.make_async_copy(rows, taken.at[step], in_sems.at[step])

    def put(group):
        tables = pl.ds(each * group, each)
        return pltpu.make_async_copy(placed.at[tables], tables_ref.at[tables], out_sems.at[group])

    for step in range(steps):
        fetch(step).start()
    for step in range(steps):
        group, half = step // halves, step % halves
        fetch(step).wait()
        rows = taken.at[step].reshape(count * each, lanes)
        for table in range(each):
            picked = rows[pl.ds(table, count, stride=each), :]
            placed[each * group + table, :, lanes * half : lanes * (half + 1)] = picked
        if half == halves - 1:
            put(group).start()
    for group in range(groups):
        put(group).wait()


def by_table(samples):
    count, _, tables, width = samples.shape
    groups, lanes = tables // 8, width // 2
    return pl.pallas_call(
        by_table_kernel,
        out_shape=jax.ShapeDtypeStruct((tables, count, width), jnp.float32),
        in_specs=[spec(pltpu.HBM)],
        out_specs=spec(pltpu.HBM),
        scratch_shapes=[
            pltpu.VMEM((2 * groups, count, 8, lanes), jnp.float32),
            pltpu.VMEM((tables, count, width), jnp.float32),
            pltpu.SemaphoreType.DMA((2 * groups,)),
            pltpu.SemaphoreType.DMA((groups,)),
        ],
        compiler_params=limit(63),
    )(samples)


def chunk_rows(place, high_ref, low_ref, upper, lower, count):
    rows = pl.ds(pl.multiple_of(place * count, count), count)
    high = high_ref[rows, :]
    low = low_ref[rows, :]
    dot = lambda a, b: jnp.dot(a, b, preferred_element_type=jnp.float32)
    both = dot(jnp.concatenate([high, low]), upper)
    return (dot(high, lower) + both[count:] + both[:count]) * 0.0625


def first_kernel(picks, high_ref, low_ref, arrived_ref, upper_ref, lower_ref, *out_refs):
    wide = arrived_ref[...]
    upper = wide.astype(jnp.bfloat16)
    lower = (wide - upper.astype(jnp.float32)).astype(jnp.bfloat16)
    upper_ref[...] = upper
    lower_ref[...] = lower
    for place, out_ref in enumerate(out_refs):
        out_ref[...] = chunk_rows(picks[place], high_ref, low_ref, upper, lower, out_ref.shape[0])


def rows_kernel(picks, high_ref, low_ref, upper_ref, lower_ref, *out_refs):
    upper = upper_ref[...]
    lower = lower_ref[...]
    for place, out_ref in enumerate(out_refs):
        out_ref[...] = chunk_rows(picks[place], high_ref, low_ref, upper, lower, out_ref.shape[0])


def first_rows(picks, high, low, arrived, count):
    bags, width = arrived.shape
    chunks = picks.shape[0]
    part = jax.ShapeDtypeStruct((bags, width), jnp.bfloat16)
    shape = jax.ShapeDtypeStruct((count, width), jnp.float32)
    return pl.pallas_call(
        first_kernel,
        out_shape=(part, part) + (shape,) * chunks,
        in_specs=[spec(SMEM)] + [spec(VMEM)] * 3,
        out_specs=(spec(VMEM),) * (2 + chunks),
        compiler_params=limit(10),
        cost_estimate=pl.CostEstimate(
            flops=6 * chunks * count * width * bags, bytes_accessed=3 << 20, transcendentals=0
        ),
    )(picks, high, low, arrived)


def grad_rows(picks, high, low, upper, lower, count):
    bags, width = upper.shape
    chunks = picks.shape[0]
    shape = jax.ShapeDtypeStruct((count, width), jnp.float32)
    return pl.pallas_call(
        rows_kernel,
        out_shape=(shape,) * chunks,
        in_specs=[spec(SMEM)] + [spec(VMEM)] * 4,
        out_specs=(spec(VMEM),) * chunks,
        compiler_params=limit(10),
        cost_estimate=pl.CostEstimate(
            flops=600 * chunks * count * width * bags, bytes_accessed=3 << 20, transcendentals=0
        ),
    )(picks, high, low, upper, lower)


def add_kernel(one_ref, two_ref, out_ref):
    out_ref[...] = one_ref[...] + two_ref[...]


def added(one, two):
    return pl.pallas_call(
        add_kernel,
        out_shape=jax.ShapeDtypeStruct(one.shape, one.dtype),
        in_specs=[spec(VMEM)] * 2,
        out_specs=spec(VMEM),
        compiler_params=limit(2),
    )(one, two)


def adagrad_kernel(pick, mine_ref, other_ref, rows_ref, state_ref, grad_ref, fresh_ref):
    count = mine_ref.shape[0]
    rows = pl.ds(pl.multiple_of(pick[0] * count, count), count)
    grads = mine_ref[...] + other_ref[...]
    grad_ref[...] = grads
    state = state_ref[rows, :] + jnp.mean(grads * grads, axis=-1, keepdims=True)
    fresh_ref[...] = rows_ref[rows, :] - learn_rate * grads / (jnp.sqrt(state) + 1e-08)


def adagrad(pick, mine, other, rows, state):
    shape = jax.ShapeDtypeStruct(mine.shape, jnp.float32)
    return pl.pallas_call(
        adagrad_kernel,
        out_shape=(shape, shape),
        in_specs=[spec(SMEM)] + [spec(VMEM)] * 4,
        out_specs=(spec(VMEM),) * 2,
        compiler_params=limit(4),
    )(pick, mine, other, rows, state)


def per_device(pooled_grad, bag_lengths, row_slots, id_weights, touched_rows, accumulator):
    reps = lax.axis_size("rep")
    shards = lax.axis_size("shard")
    height = touched_rows.shape[1]
    count = height // reps
    rep = lax.axis_index("rep")
    core = lax.axis_index("shard") % 2
    near = jnp.where(core == 0, 1, 3)

    def ordered(one, two):
        return jnp.stack([jnp.minimum(one, two), jnp.maximum(one, two)])

    keep = ordered(rep, rep ^ (near ^ 2))
    give = ordered(rep ^ near, rep ^ 2)

    def swap(array, step):
        pairs = []
        for shard in range(shards):
            turn = 1 if (shard + step) % 2 == 0 else 3
            pairs += [(shard * reps + r, shard * reps + (r ^ turn)) for r in range(reps)]
        return lax.ppermute(array, ("shard", "rep"), pairs)

    arrived = lax.all_to_all(by_table(pooled_grad), "shard", 0, 0, tiled=True)
    arrived = arrived.reshape(-1, arrived.shape[2])
    high, low = tallies(bag_lengths[0], row_slots[0], id_weights[0], height)
    state = accumulator.reshape(height, 1)
    upper, lower, one = first_rows(give[:1], high, low, arrived, count)
    (two,) = grad_rows(give[1:], high, low, upper, lower, count)
    sent = [swap(one, 0), swap(two, 0)]
    kept = grad_rows(keep, high, low, upper, lower, count)
    mine = [added(kept[k], sent[k]) for k in range(2)]
    other = [swap(piece, 1) for piece in mine]
    grads, fresh = zip(
        *[adagrad(keep[k : k + 1], mine[k], other[k], touched_rows[0], state) for k in range(2)]
    )
    far = [swap(piece, 0) for piece in fresh]
    grad = jnp.where(rep == keep[0], grads[0], grads[1])
    updated = jnp.zeros((reps, count, touched_rows.shape[2]), jnp.float32)
    for k in range(2):
        updated = lax.dynamic_update_index_in_dim(updated, fresh[k], keep[k], 0)
    for k in range(2):
        updated = lax.dynamic_update_index_in_dim(updated, far[k], give[k], 0)
    return grad[None], updated.reshape(touched_rows.shape)


def solution(mesh):
    placed = (
        P("shard", "rep", None, None),
        P("shard", "rep", None),
        P("shard", "rep", None),
        P("shard", "rep", None),
        P("shard", None, None),
        P("shard", None),
    )
    return jax.shard_map(
        per_device,
        mesh=mesh,
        in_specs=placed,
        out_specs=(P("shard", "rep", None), P("shard", None, None)),
        check_vma=False,
    )
```

```python
import functools

import jax
import jax.numpy as jnp
from jax import lax
from jax.experimental import pallas as pl
from jax.experimental.pallas import tpu as pltpu
from jax.sharding import PartitionSpec as P

learn_rate = 0.5
span = 1024
block = 256
window = 256
VMEM = pltpu.VMEM
SMEM = pltpu.SMEM


def tally_kernel(edges, starts_ref, ends_ref, slots_ref, weights_ref, high_ref, low_ref, total):
    height = total.shape[0]
    narrow = jnp.bfloat16
    half = height // 2

    def coded(slots):
        return jnp.where(slots < half, slots, half - 1 - slots).astype(jnp.float32).astype(narrow)

    slot_ids = coded(lax.broadcasted_iota(jnp.int32, (height, block), 0))
    offsets = lax.broadcasted_iota(jnp.int32, (block, window), 0).astype(jnp.float32).astype(narrow)
    zero = jnp.zeros((), narrow)
    one = jnp.ones((), narrow)
    for part in range(high_ref.shape[1] // window):
        columns = pl.ds(part * window, window)
        starts = starts_ref[:, columns]
        ends = ends_ref[:, columns]
        total[...] = jnp.zeros_like(total)

        def add_span(step, carry):
            added = jnp.zeros_like(total)
            for piece in range(span // block):
                base = pl.multiple_of(step * span + piece * block, block)

                def local(bounds):
                    return jnp.clip(bounds - base, 0, block).astype(jnp.float32).astype(narrow)

                codes = coded(slots_ref[:, pl.ds(base, block)])
                weights = weights_ref[:, pl.ds(base, block)].astype(jnp.float32).astype(narrow)
                chosen = jnp.where(slot_ids == codes, weights, zero)
                member = (offsets >= local(starts)) & (offsets < local(ends))
                added += jnp.dot(
                    chosen, jnp.where(member, one, zero), preferred_element_type=jnp.float32
                )
            total[...] += added
            return carry

        first = edges[part] // span
        last = (edges[part + 1] + span - 1) // span
        lax.fori_loop(first, last, add_span, 0)
        high = total[...].astype(narrow)
        high_ref[:, columns] = high
        low_ref[:, columns] = (total[...] - high.astype(jnp.float32)).astype(narrow)


def spec(space):
    return pl.BlockSpec(memory_space=space)


def limit(mebibytes):
    return pltpu.CompilerParams(vmem_limit_bytes=mebibytes << 20)


def tallies(lengths, slots, weights, height):
    bags = lengths.shape[1]
    ends = jnp.cumsum(lengths, axis=1)
    starts = ends - lengths
    edges = jnp.concatenate([starts[0, ::window], ends[0, -1:]])
    shape = jax.ShapeDtypeStruct((height, bags), jnp.bfloat16)
    return pl.pallas_call(
        tally_kernel,
        out_shape=(shape, shape),
        in_specs=[spec(SMEM)] + [spec(VMEM)] * 4,
        out_specs=(spec(VMEM),) * 2,
        scratch_shapes=[pltpu.VMEM((height, window), jnp.float32)],
        compiler_params=limit(10),
        cost_estimate=pl.CostEstimate(
            flops=2 * 35 * height * 512 * window, bytes_accessed=2 << 20, transcendentals=0
        ),
    )(edges, starts, ends, slots, weights)


def by_table_kernel(samples_ref, tables_ref, taken, placed, in_sems, out_sems):
    steps, _, each, lanes = taken.shape
    halves = 2
    groups = steps // halves
    count = placed.shape[1]

    def fetch(step):
        group, half = step // halves, step % halves
        rows = samples_ref.at[:, 0, pl.ds(each * group, each), pl.ds(lanes * half, lanes)]
        return pltpu.make_async_copy(rows, taken.at[step], in_sems.at[step])

    def put(group):
        tables = pl.ds(each * group, each)
        return pltpu.make_async_copy(placed.at[tables], tables_ref.at[tables], out_sems.at[group])

    for step in range(steps):
        fetch(step).start()
    for step in range(steps):
        group, half = step // halves, step % halves
        fetch(step).wait()
        rows = taken.at[step].reshape(count * each, lanes)
        for table in range(each):
            picked = rows[pl.ds(table, count, stride=each), :]
            placed[each * group + table, :, lanes * half : lanes * (half + 1)] = picked
        if half == halves - 1:
            put(group).start()
    for group in range(groups):
        put(group).wait()


def by_table(samples):
    count, _, tables, width = samples.shape
    groups, lanes = tables // 8, width // 2
    return pl.pallas_call(
        by_table_kernel,
        out_shape=jax.ShapeDtypeStruct((tables, count, width), jnp.float32),
        in_specs=[spec(pltpu.HBM)],
        out_specs=spec(pltpu.HBM),
        scratch_shapes=[
            pltpu.VMEM((2 * groups, count, 8, lanes), jnp.float32),
            pltpu.VMEM((tables, count, width), jnp.float32),
            pltpu.SemaphoreType.DMA((2 * groups,)),
            pltpu.SemaphoreType.DMA((groups,)),
        ],
        compiler_params=limit(63),
    )(samples)


def chunk_rows(place, high_ref, low_ref, upper, lower, count):
    rows = pl.ds(pl.multiple_of(place * count, count), count)
    high = high_ref[rows, :]
    low = low_ref[rows, :]
    dot = lambda a, b: jnp.dot(a, b, preferred_element_type=jnp.float32)
    both = dot(jnp.concatenate([high, low]), upper)
    return (dot(high, lower) + both[count:] + both[:count]) * 0.0625


def first_kernel(picks, high_ref, low_ref, arrived_ref, upper_ref, lower_ref, *out_refs):
    wide = arrived_ref[...]
    upper = wide.astype(jnp.bfloat16)
    lower = (wide - upper.astype(jnp.float32)).astype(jnp.bfloat16)
    upper_ref[...] = upper
    lower_ref[...] = lower
    for place, out_ref in enumerate(out_refs):
        out_ref[...] = chunk_rows(picks[place], high_ref, low_ref, upper, lower, out_ref.shape[0])


def rows_kernel(picks, high_ref, low_ref, upper_ref, lower_ref, *out_refs):
    upper = upper_ref[...]
    lower = lower_ref[...]
    for place, out_ref in enumerate(out_refs):
        out_ref[...] = chunk_rows(picks[place], high_ref, low_ref, upper, lower, out_ref.shape[0])


def first_rows(picks, high, low, arrived, count):
    bags, width = arrived.shape
    chunks = picks.shape[0]
    part = jax.ShapeDtypeStruct((bags, width), jnp.bfloat16)
    shape = jax.ShapeDtypeStruct((count, width), jnp.float32)
    return pl.pallas_call(
        first_kernel,
        out_shape=(part, part) + (shape,) * chunks,
        in_specs=[spec(SMEM)] + [spec(VMEM)] * 3,
        out_specs=(spec(VMEM),) * (2 + chunks),
        compiler_params=limit(10),
        cost_estimate=pl.CostEstimate(
            flops=6 * chunks * count * width * bags, bytes_accessed=3 << 20, transcendentals=0
        ),
    )(picks, high, low, arrived)


def grad_rows(picks, high, low, upper, lower, count):
    bags, width = upper.shape
    chunks = picks.shape[0]
    shape = jax.ShapeDtypeStruct((count, width), jnp.float32)
    return pl.pallas_call(
        rows_kernel,
        out_shape=(shape,) * chunks,
        in_specs=[spec(SMEM)] + [spec(VMEM)] * 4,
        out_specs=(spec(VMEM),) * chunks,
        compiler_params=limit(10),
        cost_estimate=pl.CostEstimate(
            flops=6 * chunks * count * width * bags, bytes_accessed=3 << 20, transcendentals=0
        ),
    )(picks, high, low, upper, lower)


def add_kernel(one_ref, two_ref, out_ref):
    out_ref[...] = one_ref[...] + two_ref[...]


def added(one, two):
    return pl.pallas_call(
        add_kernel,
        out_shape=jax.ShapeDtypeStruct(one.shape, one.dtype),
        in_specs=[spec(VMEM)] * 2,
        out_specs=spec(VMEM),
        compiler_params=limit(2),
    )(one, two)


def adagrad_kernel(pick, mine_ref, other_ref, rows_ref, state_ref, grad_ref, fresh_ref):
    count = mine_ref.shape[0]
    rows = pl.ds(pl.multiple_of(pick[0] * count, count), count)
    grads = mine_ref[...] + other_ref[...]
    grad_ref[...] = grads
    state = state_ref[rows, :] + jnp.mean(grads * grads, axis=-1, keepdims=True)
    fresh_ref[...] = rows_ref[rows, :] - learn_rate * grads / (jnp.sqrt(state) + 1e-08)


def adagrad(pick, mine, other, rows, state):
    shape = jax.ShapeDtypeStruct(mine.shape, jnp.float32)
    return pl.pallas_call(
        adagrad_kernel,
        out_shape=(shape, shape),
        in_specs=[spec(SMEM)] + [spec(VMEM)] * 4,
        out_specs=(spec(VMEM),) * 2,
        compiler_params=limit(4),
    )(pick, mine, other, rows, state)


def place_kernel(count, picks, *refs):
    pieces, out_ref, sems = refs[:count], refs[-2], refs[-1]
    copies = []
    for k, piece in enumerate(pieces):
        rows = piece.shape[0]
        start = pl.multiple_of(picks[k] * rows, rows)
        copies.append(
            pltpu.make_async_copy(piece, out_ref.at[0, pl.ds(start, rows)], sems.at[k])
        )
    for copy in copies:
        copy.start()
    for copy in copies:
        copy.wait()


def placed_rows(picks, pieces, shape, into=None):
    count = len(pieces)
    rest = () if into is None else (into,)
    return pl.pallas_call(
        functools.partial(place_kernel, count),
        out_shape=jax.ShapeDtypeStruct(shape, jnp.float32),
        in_specs=[spec(SMEM)] + [spec(VMEM)] * count + [spec(pl.ANY)] * len(rest),
        out_specs=spec(pl.ANY),
        scratch_shapes=[pltpu.SemaphoreType.DMA((count,))],
        input_output_aliases={} if into is None else {1 + count: 0},
        compiler_params=limit(2),
    )(picks, *pieces, *rest)


def per_device(pooled_grad, bag_lengths, row_slots, id_weights, touched_rows, accumulator):
    reps = lax.axis_size("rep")
    shards = lax.axis_size("shard")
    height = touched_rows.shape[1]
    count = height // reps
    rep = lax.axis_index("rep")
    core = lax.axis_index("shard") % 2
    near = jnp.where(core == 0, 1, 3)

    def ordered(one, two):
        return jnp.stack([jnp.minimum(one, two), jnp.maximum(one, two)])

    keep = ordered(rep, rep ^ (near ^ 2))
    give = ordered(rep ^ near, rep ^ 2)

    def swap(array, step):
        pairs = []
        for shard in range(shards):
            turn = 1 if (shard + step) % 2 == 0 else 3
            pairs += [(shard * reps + r, shard * reps + (r ^ turn)) for r in range(reps)]
        return lax.ppermute(array, ("shard", "rep"), pairs)

    arrived = lax.all_to_all(by_table(pooled_grad), "shard", 0, 0, tiled=True)
    arrived = arrived.reshape(-1, arrived.shape[2])
    high, low = tallies(bag_lengths[0], row_slots[0], id_weights[0], height)
    state = accumulator.reshape(height, 1)
    upper, lower, two = first_rows(give[1:], high, low, arrived, count)
    (one,) = grad_rows(give[:1], high, low, upper, lower, count)
    sent = [swap(one, 0), swap(two, 0)]
    kept = grad_rows(keep, high, low, upper, lower, count)
    mine = [added(kept[k], sent[k]) for k in range(2)]
    other = [swap(piece, 1) for piece in mine]
    grads, fresh = zip(
        *[adagrad(keep[k : k + 1], mine[k], other[k], touched_rows[0], state) for k in range(2)]
    )
    far = [swap(piece, 0) for piece in fresh]
    grad = jnp.where(rep == keep[0], grads[0], grads[1])
    places = jnp.concatenate([keep, give[:1]])
    updated = placed_rows(places, (*fresh, far[0]), touched_rows.shape)
    updated = placed_rows(give[1:], (far[1],), touched_rows.shape, updated)
    return grad[None], updated


def solution(mesh):
    placed = (
        P("shard", "rep", None, None),
        P("shard", "rep", None),
        P("shard", "rep", None),
        P("shard", "rep", None),
        P("shard", None, None),
        P("shard", None),
    )
    return jax.shard_map(
        per_device,
        mesh=mesh,
        in_specs=placed,
        out_specs=(P("shard", "rep", None), P("shard", None, None)),
        check_vma=False,
    )
```
